256 devices in a mesh: kvh: 8 (over y, core), seq: 32 (over x, z).
Axes of the slice: x: 4, y: 4, z: 8, core: 2. Of those that a mesh axis runs over, the one named last changes fastest.
Arguments:
- queries: bfloat16 [16, 128, 128], P(None, 'kvh'), may hold values from -20 to 20
- token_keys: bfloat16 [16, 8, 128], P(None, 'kvh'), may hold values from -6 to 6
- token_values: bfloat16 [16, 8, 128], P(None, 'kvh'), may hold values from -6 to 6
- key_cache: bfloat16 [16, 4096, 8, 128], P(None, 'seq', 'kvh'), may hold values from -20 to 20
- cached_value_rows: bfloat16 [16, 4096, 8, 128], P(None, 'seq', 'kvh'), may hold values from -6 to 6
- lengths: int32 [16], replicated, may hold values from 1024 to 4096, as said below
- residual: bfloat16 [16, 16384], P(None, 'seq'), may hold values from -7 to 7
- out_weight: bfloat16 [16384, 16384], P('kvh', 'seq'), may hold values from -0.1875 to 0.1875
- norm_gain: bfloat16 [16384], P('seq'), may hold values from 0.099609375 to 1.8984375
- gate_weight: bfloat16 [16384, 26624], P('seq', 'kvh'), may hold values from -0.046875 to 0.046875
- up_weight: bfloat16 [16384, 26624], P('seq', 'kvh'), may hold values from -0.046875 to 0.046875
- down_weight: bfloat16 [26624, 16384], P('kvh', 'seq'), may hold values from -0.0390625 to 0.0390625
Outputs:
- updated: bfloat16 [16, 16384], P(None, 'seq')
- attended: bfloat16 [16, 16384], P(None, 'kvh')
The draws below stay inside these ranges and needn't reach their ends.
Inputs may be any that keep to these rules, and one draw needn't show every extreme that they name: Each request's cached tokens fill slots 0 to lengths - 1; some request has exactly 4096 and some exactly 1024.
All inputs are finite; a program needn't handle non-finite values.
Results may differ from the reference program's by a relative error of at most 0.008.
Values may be sent and summed in bfloat16 or wider, within the bound.
No kernel may reach another device: no remote copies, remote signals or barrier semaphores. Data moves between devices by JAX's collectives and lax.ppermute only.
A program may use at most 64 MiB of HBM per device.

```python
import jax
import jax.numpy as jnp
from jax import lax

D = 16384
QUERY_HEADS = 128
KEY_VALUE_HEADS = 8
HEAD_DIMENSION = 128
FFW = 26624
REQUEST_COUNT = 16
SLOT_DEV = 128
CONTEXT_SLOTS = 4096


def draw_queries(key, part):
    key = jax.random.fold_in(key, 1)
    sampled_values = 1.5 * jnp.clip(jax.random.normal(key, (REQUEST_COUNT, QUERY_HEADS, HEAD_DIMENSION), jnp.float32), -6.0, 6.0)
    return sampled_values.astype(jnp.bfloat16)


def draw_key_cache(key, part):
    key = jax.random.fold_in(key, 2)
    sampled_values = jnp.clip(jax.random.normal(key, (REQUEST_COUNT, CONTEXT_SLOTS, KEY_VALUE_HEADS, HEAD_DIMENSION), jnp.float32), -6.0, 6.0)
    return sampled_values.astype(jnp.bfloat16)


def draw_lengths(key, part):
    key = jax.random.fold_in(key, 3)
    drawn = jax.random.randint(key, (REQUEST_COUNT,), CONTEXT_SLOTS // 4, CONTEXT_SLOTS + 1)
    order = jax.random.permutation(jax.random.fold_in(key, 5), REQUEST_COUNT)
    drawn = drawn.at[order[0]].set(CONTEXT_SLOTS).at[order[1]].set(CONTEXT_SLOTS // 4)
    return drawn.astype(jnp.int32)


def draw_residual(key, part):
    key = jax.random.fold_in(key, 4)
    column_scale = 0.3 + 0.6 * jnp.arange(D, dtype=jnp.float32) / D
    sampled_values = jnp.clip(jax.random.normal(key, (REQUEST_COUNT, D), jnp.float32), -4.0, 4.0) * column_scale
    return sampled_values.astype(jnp.bfloat16)


def block_levels(key, dims, cuts, least, top_value):
    gain, own = 1.0, jax.random.fold_in(key, 6)
    for position, shards_of in cuts:
        heights = jnp.exp(jax.random.uniform(jax.random.fold_in(own, position), (shards_of,), jnp.float32, least / len(cuts), top_value / len(cuts)))
        gain = gain * jnp.repeat(heights, dims[position] // shards_of).reshape([-1 if axis == position else 1 for axis in range(len(dims))])
    return gain


def bell_draw(own_key, dims, scale, bound, shards=(), kind=jnp.bfloat16):
    values = scale * jax.random.normal(own_key, dims, jnp.float32)
    if shards:
        values = values * block_levels(own_key, dims, shards, -0.22, 0.18)
    return jnp.clip(values, -bound, bound).astype(kind)


def setup_inputs(seed: int = 0) -> dict:
    splits = jax.random.split(jax.random.key(seed), 13)
    return {
        "queries": draw_queries(jax.random.fold_in(splits[12], 71), 0),
        "token_keys": bell_draw(splits[1], (REQUEST_COUNT, KEY_VALUE_HEADS, HEAD_DIMENSION), 1.0, 6.0, ((1, 8),)),
        "token_values": bell_draw(splits[2], (REQUEST_COUNT, KEY_VALUE_HEADS, HEAD_DIMENSION), 1.0, 6.0, ((1, 8),)),
        "key_cache": draw_key_cache(jax.random.fold_in(splits[12], 71), 0),
        "cached_value_rows": bell_draw(splits[4], (REQUEST_COUNT, CONTEXT_SLOTS, KEY_VALUE_HEADS, HEAD_DIMENSION), 1.0, 6.0, ((1, 32), (2, 8))),
        "lengths": draw_lengths(jax.random.fold_in(splits[12], 71), 0),
        "residual": draw_residual(jax.random.fold_in(splits[12], 71), 0),
        "out_weight": bell_draw(splits[7], (QUERY_HEADS * HEAD_DIMENSION, D), (QUERY_HEADS * HEAD_DIMENSION // 16) ** -0.5, 0.1875, ((0, 8), (1, 32))),
        "norm_gain": jnp.clip(1.0 + 0.18 * jax.random.normal(splits[8], (D,), jnp.float32), 0.099609375, 1.8984375).astype(jnp.bfloat16),
        "gate_weight": bell_draw(splits[9], (D, FFW), D ** -0.5, 0.046875, ((0, 32), (1, 8))),
        "up_weight": bell_draw(splits[10], (D, FFW), D ** -0.5, 0.046875, ((0, 32), (1, 8))),
        "down_weight": bell_draw(splits[11], (FFW, D), FFW ** -0.5, 0.0390625, ((0, 8), (1, 32))),
    }


def reference(queries, token_keys, token_values, key_cache, cached_value_rows, lengths, residual, out_weight, norm_gain, gate_weight, up_weight, down_weight):
    query_groups = QUERY_HEADS // KEY_VALUE_HEADS
    score_scale = HEAD_DIMENSION ** (-0.5)
    block_count = CONTEXT_SLOTS // SLOT_DEV

    def one_request(inputs):
        query_input, keys, values, new_key, new_value, length = inputs
        query_input = query_input.astype(jnp.float32).reshape(KEY_VALUE_HEADS, query_groups, HEAD_DIMENSION)
        scores = jnp.einsum('hgd,chd->hgc', query_input, keys.astype(jnp.float32)) * score_scale
        scores = scores.reshape(KEY_VALUE_HEADS, query_groups, block_count, SLOT_DEV)
        is_valid = (jnp.arange(CONTEXT_SLOTS) < length).reshape(block_count, SLOT_DEV)
        fresh_score = jnp.einsum('hgd,hd->hg', query_input, new_key.astype(jnp.float32)) * score_scale
        scores = jnp.where(is_valid, scores, -1e+30)
        first_block = jnp.arange(block_count) == 0
        block_peak = lax.optimization_barrier(jnp.max(scores, -1))
        block_peak = jnp.where(first_block, jnp.maximum(block_peak, fresh_score[..., None]), block_peak)
        weights = jnp.where(is_valid, jnp.exp(scores - block_peak[..., None]), 0.0)
        own_weight = jnp.exp(fresh_score - block_peak[..., 0])
        block_total = lax.optimization_barrier(jnp.sum(weights, -1))
        block_total = block_total.at[..., 0].add(own_weight)
        rounded = lax.optimization_barrier(weights.astype(jnp.bfloat16)).astype(jnp.float32)
        own_rounded = lax.optimization_barrier(own_weight.astype(jnp.bfloat16)).astype(jnp.float32)
        value_blocks = values.astype(jnp.float32).reshape(block_count, SLOT_DEV, KEY_VALUE_HEADS, HEAD_DIMENSION)
        block_acc = jnp.einsum('hgns,nshd->hgnd', rounded, value_blocks)
        block_acc = block_acc.at[:, :, 0, :].add(own_rounded[..., None] * new_value.astype(jnp.float32)[:, None, :])
        top_peak = lax.optimization_barrier(jnp.max(block_peak, -1))
        factors = jnp.exp(block_peak - top_peak[..., None])
        total_sum = lax.optimization_barrier(jnp.sum(block_total * factors, -1))
        mixed = lax.optimization_barrier(jnp.sum(block_acc * factors[..., None], 2))
        return (mixed / total_sum[..., None]).astype(jnp.bfloat16).reshape(QUERY_HEADS * HEAD_DIMENSION)
    attended = lax.map(one_request, (queries, key_cache, cached_value_rows, token_keys, token_values, lengths))
    projected = jnp.dot(attended, out_weight, preferred_element_type=jnp.float32)
    middle = (residual.astype(jnp.float32) + projected).astype(jnp.bfloat16)
    wide = middle.astype(jnp.float32)
    mean_square = lax.optimization_barrier(jnp.mean(wide * wide, -1))
    normed = (wide * lax.rsqrt(mean_square + 1e-05)[:, None] * norm_gain.astype(jnp.float32)).astype(jnp.bfloat16)
    gate_proj = jnp.dot(normed, gate_weight, preferred_element_type=jnp.float32)
    up_proj = jnp.dot(normed, up_weight, preferred_element_type=jnp.float32)
    hidden = (jax.nn.silu(gate_proj) * up_proj).astype(jnp.bfloat16)
    down_proj = jnp.dot(hidden, down_weight, preferred_element_type=jnp.float32)
    updated = (wide + down_proj).astype(jnp.bfloat16)
    return (updated, attended)
```

```python
import jax
import jax.numpy as jnp
from jax import lax
from jax.experimental import pallas as pl
from jax.experimental.pallas import tpu as pltpu
from jax.sharding import PartitionSpec as P

D = 16384
BF = jnp.bfloat16
F32 = jnp.float32
LANES = 128
MIB = 1 << 20
KEY_PARTS = 4
VMEM = pl.BlockSpec(memory_space=pltpu.VMEM)
SMEM = pl.BlockSpec(memory_space=pltpu.SMEM)
HBM = pl.BlockSpec(memory_space=pltpu.HBM)
DMA = pltpu.SemaphoreType.DMA


def call(body, out_shape, n_in, scratch=(), smem=(), hbm=(), limit=16 * MIB):
    kernel = pl.pallas_call(
        body,
        out_shape=out_shape,
        in_specs=[SMEM if i in smem else HBM if i in hbm else VMEM for i in range(n_in)],
        out_specs=jax.tree.map(lambda _: VMEM, out_shape),
        scratch_shapes=list(scratch),
        compiler_params=pltpu.CompilerParams(vmem_limit_bytes=limit),
    )

    def run(*args):
        return kernel(
            *[
                pltpu.with_memory_space_constraint(arg, pltpu.HBM) if i in hbm else arg
                for i, arg in enumerate(args)
            ]
        )

    return run


def bf(*shape):
    return jax.ShapeDtypeStruct(shape, BF)


def round_bf(value):
    return value.astype(BF).astype(F32)


def lane_index(shape):
    return lax.broadcasted_iota(jnp.int32, shape, len(shape) - 1)


def stat_rows(columns):
    rows = columns[0].shape[0]
    lane = lane_index((rows, LANES))
    out = jnp.zeros((rows, LANES), F32)
    for index, column in enumerate(columns):
        out = jnp.where(lane == index, column, out)
    return out


def two_parts(value):
    high = round_bf(value)
    return high, value - high


def start_copies(sources, targets, sems):
    copies = [
        pltpu.make_async_copy(source, target, sems.at[i])
        for i, (source, target) in enumerate(zip(sources, targets))
    ]
    for copy in copies:
        copy.start()
    return copies


def attention_kernel(where_ref, *refs):
    sources, refs = refs[:8], refs[-12:]
    out_ref, kept_ref, row_ref = refs[:3]
    targets, sems = refs[3:11], refs[11]
    len_ref, q_ref, tk_ref, k_ref, tv_ref, v_ref, res_ref, gn_ref = targets
    chunk = k_ref.shape[0] // KEY_PARTS
    chunks = [pl.ds(i * chunk, chunk) for i in range(KEY_PARTS)]
    copies = start_copies(
        [*sources[:3], *(sources[3].at[c] for c in chunks), *sources[4:]],
        [*targets[:3], *(targets[3].at[c] for c in chunks), *targets[4:]],
        sems,
    )
    for copy in copies[:3]:
        copy.wait()
    keys, others = copies[3 : 3 + KEY_PARTS], copies[3 + KEY_PARTS :]
    requests, heads, size = q_ref.shape
    slots = k_ref.shape[1]
    scale = size ** (-0.5)
    first = where_ref[0] * slots
    owner = where_ref[0] == 0
    contract = (((1,), (1,)), ((), ()))
    slot = first + lane_index((heads, slots))
    scores, valid, fresh = [], [], []
    for b in range(requests):
        if b % chunk == 0:
            keys[b // chunk].wait()
        q = q_ref[b]
        scores.append(lax.dot_general(q, k_ref[b], contract, preferred_element_type=F32))
        valid.append(jnp.where(slot < len_ref[b], 1.0, 0.0))
        fresh.append(q.astype(F32) * tk_ref[b : b + 1, :].astype(F32))
    valid = jnp.concatenate(valid, 0) > 0.5
    scores = jnp.where(valid, jnp.concatenate(scores, 0) * scale, -1e30)
    fresh = jnp.sum(jnp.concatenate(fresh, 0), -1, keepdims=True) * scale
    fresh = jnp.where(owner, fresh, -1e30)
    peak = round_bf(jnp.maximum(jnp.max(scores, -1, keepdims=True), fresh))
    weights = jnp.where(valid, jnp.exp(scores - peak), 0.0)
    own = jnp.where(owner, jnp.exp(fresh - peak), 0.0)
    total = jnp.sum(weights, -1, keepdims=True) + own
    rounded = weights.astype(BF)
    own = round_bf(own)
    stats = stat_rows((peak,) + two_parts(total)).astype(BF)
    for copy in others:
        copy.wait()
    for b in range(requests):
        rows = slice(b * heads, (b + 1) * heads)
        acc = jnp.dot(rounded[rows], v_ref[b], preferred_element_type=F32)
        acc = acc + own[rows] * tv_ref[b : b + 1, :].astype(F32)
        out_ref[b, :, :size] = acc.astype(BF)
        out_ref[b, :, size:] = stats[rows]
    kept_ref[...] = res_ref[...]
    gain = gn_ref[...].astype(F32)
    row_ref[...] = jnp.concatenate([gain[i : i + 1] for i in range(gain.shape[0])], -1)


def merge_kernel(got_ref, out_ref):
    size = out_ref.shape[-1]
    stats = got_ref[:, :, size:].astype(F32)
    peak = stats[:, :, 0:1]
    factor = jnp.exp(peak - jnp.max(peak, 0, keepdims=True))
    total = jnp.sum((stats[:, :, 1:2] + stats[:, :, 2:3]) * factor, 0)
    acc = jnp.sum(got_ref[:, :, :size].astype(F32) * factor, 0)
    out_ref[...] = jnp.broadcast_to((acc / total).astype(BF)[None], out_ref.shape)


def project_kernel(got_ref, weight_ref, attended_ref, out_ref, rows_ref):
    requests = attended_ref.shape[0]
    heads = rows_ref.shape[0] // requests
    rows_ref[...] = got_ref[...].astype(F32).reshape(rows_ref.shape)
    attended = jnp.concatenate(
        [rows_ref[pl.ds(h, requests, stride=heads), :].astype(BF) for h in range(heads)], -1
    )
    attended_ref[...] = attended
    projected = jnp.dot(attended, weight_ref[...], preferred_element_type=F32)
    out_ref[...] = jnp.broadcast_to(projected.astype(BF)[None], out_ref.shape)


def gate_up_kernel(
    got_ref, residual_ref, gain_ref, gate_ref, up_ref, middle_ref, out_ref, rows_ref
):
    pieces, depth, _ = out_ref.shape
    requests = residual_ref.shape[0]
    halves = pieces // requests
    projected = jnp.sum(got_ref[...].astype(F32), 0)
    middle = (residual_ref[...].astype(F32) + projected).astype(BF)
    middle_ref[...] = middle
    middle = middle.astype(F32)
    square = jnp.sum(middle * middle, -1, keepdims=True)
    scaled = (middle * gain_ref[...]).astype(BF)
    blocks = gate_ref.shape[1] // (halves * LANES)

    def put(row, half, value):
        rows_ref[pl.ds(half * depth + row, requests, stride=halves * depth), :] = value

    for start, weight_ref in ((0, gate_ref), (blocks, up_ref)):
        product = jnp.dot(scaled, weight_ref[...], preferred_element_type=F32)
        for j in range(halves * blocks):
            put(start + j % blocks, j // blocks, product[:, j * LANES : (j + 1) * LANES])
    stats = stat_rows(two_parts(square))
    zeros = jnp.zeros_like(stats)
    for half in range(halves):
        put(2 * blocks, half, stats)
        for row in range(2 * blocks + 1, depth):
            put(row, half, zeros)
    out_ref[...] = rows_ref[...].astype(BF).reshape(out_ref.shape)


def hidden_kernel(blocks, got_ref, out_ref):
    summed = jnp.sum(got_ref[...].astype(F32), 0)
    stats = summed[2 * blocks : 2 * blocks + 1]
    square = stats[:, 0:1] + stats[:, 1:2]
    inverse = lax.rsqrt(square / D + 1e-05)
    gate = summed[:blocks] * inverse
    up = summed[blocks : 2 * blocks] * inverse
    hidden = gate / (1.0 + jnp.exp(-gate)) * up
    pad = jnp.zeros((out_ref.shape[1] - blocks, LANES), F32)
    hidden = jnp.concatenate([hidden, pad], 0).astype(BF)
    out_ref[...] = jnp.broadcast_to(hidden[None], out_ref.shape)


def down_kernel(got_ref, weight_ref, out_ref, rows_ref):
    pieces, depth, _ = got_ref.shape
    requests = out_ref.shape[1]
    halves = pieces // requests
    blocks = weight_ref.shape[0] // (halves * LANES)
    rows_ref[...] = got_ref[...].astype(F32).reshape(rows_ref.shape)
    hidden = jnp.concatenate(
        [
            rows_ref[pl.ds(half * depth + row, requests, stride=halves * depth), :].astype(BF)
            for half in range(halves)
            for row in range(blocks)
        ],
        -1,
    )
    down = jnp.dot(hidden, weight_ref[...], preferred_element_type=F32)
    out_ref[...] = jnp.broadcast_to(down.astype(BF)[None], out_ref.shape)


def finish_kernel(got_ref, middle_ref, out_ref):
    down = jnp.sum(got_ref[...].astype(F32), 0)
    out_ref[...] = (middle_ref[...].astype(F32) + down).astype(BF)


def exchange(pieces, axis):
    return lax.all_to_all(pieces, axis, 0, 0)


def shards(
    queries,
    token_keys,
    token_values,
    key_cache,
    cached_value_rows,
    lengths,
    residual,
    out_weight,
    norm_gain,
    gate_weight,
    up_weight,
    down_weight,
):
    requests, heads, size = queries.shape
    seq, kvh = lax.axis_size("seq"), lax.axis_size("kvh")
    rows = requests * heads // seq
    width = residual.shape[1]
    halves = seq // requests
    blocks = gate_weight.shape[1] // (halves * LANES)
    depth = -(-(2 * blocks + 1) // 16) * 16
    thin = -(-blocks // 16) * 16
    where = lax.axis_index("seq").reshape(1)

    cache = (requests, key_cache.shape[1], size)
    packed, residual, gain = call(
        attention_kernel,
        (
            bf(requests, heads, 2 * size),
            bf(requests, width),
            jax.ShapeDtypeStruct((1, width), F32),
        ),
        12,
        scratch=[
            pltpu.SMEM((requests,), jnp.int32),
            pltpu.VMEM((requests, heads, size), BF),
            pltpu.VMEM((requests, size), BF),
            pltpu.VMEM(cache, BF),
            pltpu.VMEM((requests, size), BF),
            pltpu.VMEM(cache, BF),
            pltpu.VMEM((requests, width), BF),
            pltpu.VMEM((width // LANES, LANES), BF),
            DMA((7 + KEY_PARTS,)),
        ],
        smem=(0,),
        hbm=range(1, 12),
    )(
        where,
        lengths,
        queries,
        token_keys.reshape(requests, size),
        key_cache.reshape(cache),
        token_values.reshape(requests, size),
        cached_value_rows.reshape(cache),
        residual,
        norm_gain.reshape(-1, LANES),
        gate_weight,
        up_weight,
        down_weight,
    )
    got = exchange(packed.reshape(seq, rows, 2 * size), "seq")
    merged = call(merge_kernel, bf(seq, rows, size), 1)(got)
    attended, projected = call(
        project_kernel,
        (bf(requests, heads * size), bf(kvh, requests, width)),
        2,
        scratch=[pltpu.VMEM((requests * heads, size), F32)],
    )(exchange(merged, "seq"), out_weight)
    middle, pieces = call(
        gate_up_kernel,
        (bf(requests, width), bf(seq, depth, LANES)),
        5,
        scratch=[
            pltpu.VMEM((seq * depth, LANES), F32),
        ],
    )(exchange(projected, "kvh"), residual, gain, gate_weight, up_weight)
    hidden = call(lambda *refs: hidden_kernel(blocks, *refs), bf(seq, thin, LANES), 1)(
        exchange(pieces, "seq")
    )
    down = call(
        down_kernel,
        bf(kvh, requests, width),
        2,
        scratch=[pltpu.VMEM((seq * thin, LANES), F32)],
    )(exchange(hidden, "seq"), down_weight)
    updated = call(finish_kernel, bf(requests, width), 2)(exchange(down, "kvh"), middle)
    return (updated, attended)


def solution(mesh):
    return jax.shard_map(
        shards,
        mesh=mesh,
        in_specs=(
            P(None, "kvh", None),
            P(None, "kvh", None),
            P(None, "kvh", None),
            P(None, "seq", "kvh", None),
            P(None, "seq", "kvh", None),
            P(),
            P(None, "seq"),
            P("kvh", "seq"),
            P("seq"),
            P("seq", "kvh"),
            P("seq", "kvh"),
            P("kvh", "seq"),
        ),
        out_specs=(P(None, "seq"), P(None, "kvh")),
        check_vma=False,
    )
```

```python
import jax
import jax.numpy as jnp
from jax import lax
from jax.experimental import pallas as pl
from jax.experimental.pallas import tpu as pltpu
from jax.sharding import PartitionSpec as P

D = 16384
BF = jnp.bfloat16
F32 = jnp.float32
LANES = 128
MIB = 1 << 20
CORES = 2
VMEM = pl.BlockSpec(memory_space=pltpu.VMEM)
SMEM = pl.BlockSpec(memory_space=pltpu.SMEM)
HBM = pl.BlockSpec(memory_space=pltpu.HBM)
DMA = pltpu.SemaphoreType.DMA


def call(body, out_shape, n_in, scratch=(), smem=(), hbm=(), limit=16 * MIB):
    kernel = pl.pallas_call(
        body,
        out_shape=out_shape,
        in_specs=[SMEM if i in smem else HBM if i in hbm else VMEM for i in range(n_in)],
        out_specs=jax.tree.map(lambda _: VMEM, out_shape),
        scratch_shapes=list(scratch),
        compiler_params=pltpu.CompilerParams(vmem_limit_bytes=limit),
    )

    def run(*args):
        return kernel(
            *[
                pltpu.with_memory_space_constraint(arg, pltpu.HBM) if i in hbm else arg
                for i, arg in enumerate(args)
            ]
        )

    return run


def bf(*shape):
    return jax.ShapeDtypeStruct(shape, BF)


def round_bf(value):
    return value.astype(BF).astype(F32)


def lane_index(shape):
    return lax.broadcasted_iota(jnp.int32, shape, len(shape) - 1)


def stat_rows(columns):
    rows = columns[0].shape[0]
    lane = lane_index((rows, LANES))
    out = jnp.zeros((rows, LANES), F32)
    for index, column in enumerate(columns):
        out = jnp.where(lane == index, column, out)
    return out


def two_parts(value):
    high = round_bf(value)
    return high, value - high


def start_copies(sources, targets, sems):
    copies = [
        pltpu.make_async_copy(source, target, sems.at[i])
        for i, (source, target) in enumerate(zip(sources, targets))
    ]
    for copy in copies:
        copy.start()
    return copies


def attention_kernel(where_ref, *refs):
    sources, refs = refs[:8], refs[-12:]
    out_ref, kept_ref, row_ref = refs[:3]
    targets, sems = refs[3:11], refs[11]
    len_ref, q_ref, tk_ref, k_ref, tv_ref, v_ref, res_ref, gn_ref = targets
    copies = start_copies(sources, targets, sems)
    for copy in copies[:4]:
        copy.wait()
    requests, heads, size = q_ref.shape
    slots = k_ref.shape[1]
    scale = size ** (-0.5)
    first = where_ref[0] * slots
    owner = where_ref[0] == 0
    contract = (((1,), (1,)), ((), ()))
    slot = first + lane_index((heads, slots))
    scores, valid, fresh = [], [], []
    for b in range(requests):
        q = q_ref[b]
        scores.append(lax.dot_general(q, k_ref[b], contract, preferred_element_type=F32))
        valid.append(jnp.where(slot < len_ref[b], 1.0, 0.0))
        fresh.append(q.astype(F32) * tk_ref[b : b + 1, :].astype(F32))
    valid = jnp.concatenate(valid, 0) > 0.5
    scores = jnp.where(valid, jnp.concatenate(scores, 0) * scale, -1e30)
    fresh = jnp.sum(jnp.concatenate(fresh, 0), -1, keepdims=True) * scale
    fresh = jnp.where(owner, fresh, -1e30)
    peak = round_bf(jnp.maximum(jnp.max(scores, -1, keepdims=True), fresh))
    weights = jnp.where(valid, jnp.exp(scores - peak), 0.0)
    own = jnp.where(owner, jnp.exp(fresh - peak), 0.0)
    total = jnp.sum(weights, -1, keepdims=True) + own
    rounded = weights.astype(BF)
    own = round_bf(own)
    stats = stat_rows((peak,) + two_parts(total)).astype(BF)
    for copy in copies[4:]:
        copy.wait()
    for b in range(requests):
        rows = slice(b * heads, (b + 1) * heads)
        acc = jnp.dot(rounded[rows], v_ref[b], preferred_element_type=F32)
        acc = acc + own[rows] * tv_ref[b : b + 1, :].astype(F32)
        out_ref[b, :, :size] = acc.astype(BF)
        out_ref[b, :, size:] = stats[rows]
    kept_ref[...] = res_ref[...]
    gain = gn_ref[...].astype(F32)
    row_ref[...] = jnp.concatenate([gain[i : i + 1] for i in range(gain.shape[0])], -1)


def merge_kernel(got_ref, out_ref):
    size = out_ref.shape[-1]
    stats = got_ref[:, :, size:].astype(F32)
    peak = stats[:, :, 0:1]
    factor = jnp.exp(peak - jnp.max(peak, 0, keepdims=True))
    total = jnp.sum((stats[:, :, 1:2] + stats[:, :, 2:3]) * factor, 0)
    acc = jnp.sum(got_ref[:, :, :size].astype(F32) * factor, 0)
    out_ref[...] = jnp.broadcast_to((acc / total).astype(BF)[None], out_ref.shape)


def project_kernel(got_ref, weight_ref, attended_ref, out_ref, rows_ref):
    requests = attended_ref.shape[0]
    heads = rows_ref.shape[0] // requests
    rows_ref[...] = got_ref[...].astype(F32).reshape(rows_ref.shape)
    attended = jnp.concatenate(
        [rows_ref[pl.ds(h, requests, stride=heads), :].astype(BF) for h in range(heads)], -1
    )
    attended_ref[...] = attended
    projected = jnp.dot(attended, weight_ref[...], preferred_element_type=F32)
    out_ref[...] = projected.astype(BF)


def gate_up_kernel(
    got_ref, residual_ref, gain_ref, gate_ref, up_ref, middle_ref, out_ref, rows_ref
):
    pieces, depth, _ = out_ref.shape
    requests = residual_ref.shape[0]
    halves = pieces // requests
    projected = jnp.sum(got_ref[...].astype(F32), 0)
    middle = (residual_ref[...].astype(F32) + projected).astype(BF)
    middle_ref[...] = middle
    middle = middle.astype(F32)
    square = jnp.sum(middle * middle, -1, keepdims=True)
    scaled = (middle * gain_ref[...]).astype(BF)
    blocks = gate_ref.shape[1] // (halves * LANES)

    def put(row, half, value):
        rows_ref[pl.ds(half * depth + row, requests, stride=halves * depth), :] = value

    for start, weight_ref in ((0, gate_ref), (blocks, up_ref)):
        product = jnp.dot(scaled, weight_ref[...], preferred_element_type=F32)
        for j in range(halves * blocks):
            put(start + j % blocks, j // blocks, product[:, j * LANES : (j + 1) * LANES])
    stats = stat_rows(two_parts(square))
    zeros = jnp.zeros_like(stats)
    for half in range(halves):
        put(2 * blocks, half, stats)
        for row in range(2 * blocks + 1, depth):
            put(row, half, zeros)
    out_ref[...] = rows_ref[...].astype(BF).reshape(out_ref.shape)


def hidden_kernel(blocks, got_ref, out_ref):
    summed = jnp.sum(got_ref[...].astype(F32), 0)
    stats = summed[2 * blocks : 2 * blocks + 1]
    square = stats[:, 0:1] + stats[:, 1:2]
    inverse = lax.rsqrt(square / D + 1e-05)
    gate = summed[:blocks] * inverse
    up = summed[blocks : 2 * blocks] * inverse
    hidden = gate / (1.0 + jnp.exp(-gate)) * up
    pad = jnp.zeros((out_ref.shape[1] - blocks, LANES), F32)
    hidden = jnp.concatenate([hidden, pad], 0).astype(BF)
    out_ref[...] = jnp.broadcast_to(hidden[None], out_ref.shape)


def down_kernel(got_ref, weight_ref, out_ref, rows_ref):
    pieces, depth, _ = got_ref.shape
    requests = out_ref.shape[0]
    halves = pieces // requests
    blocks = weight_ref.shape[0] // (halves * LANES)
    rows_ref[...] = got_ref[...].astype(F32).reshape(rows_ref.shape)
    hidden = jnp.concatenate(
        [
            rows_ref[pl.ds(half * depth + row, requests, stride=halves * depth), :].astype(BF)
            for half in range(halves)
            for row in range(blocks)
        ],
        -1,
    )
    down = jnp.dot(hidden, weight_ref[...], preferred_element_type=F32)
    out_ref[...] = down.astype(BF)


def finish_kernel(got_ref, middle_ref, out_ref):
    down = jnp.sum(got_ref[...].astype(F32), 0)
    out_ref[...] = (middle_ref[...].astype(F32) + down).astype(BF)


def add_kernel(a_ref, b_ref, out_ref):
    total = (a_ref[...].astype(F32) + b_ref[...].astype(F32)).astype(BF)
    out_ref[...] = jnp.broadcast_to(total[None], out_ref.shape)


def exchange(pieces, axis):
    return lax.all_to_all(pieces, axis, 0, 0)


def parts_kvh(value):
    size = lax.axis_size("kvh")
    other = lax.ppermute(value, "kvh", [(i, i ^ 1) for i in range(size)])
    both = call(add_kernel, bf(size // CORES, *value.shape), 2)(value, other)
    columns = [list(range(core, size, CORES)) for core in range(CORES)]
    return lax.all_to_all(both, "kvh", 0, 0, axis_index_groups=columns)


def shards(
    queries,
    token_keys,
    token_values,
    key_cache,
    cached_value_rows,
    lengths,
    residual,
    out_weight,
    norm_gain,
    gate_weight,
    up_weight,
    down_weight,
):
    requests, heads, size = queries.shape
    seq = lax.axis_size("seq")
    rows = requests * heads // seq
    width = residual.shape[1]
    halves = seq // requests
    blocks = gate_weight.shape[1] // (halves * LANES)
    depth = -(-(2 * blocks + 1) // 16) * 16
    thin = -(-blocks // 16) * 16
    where = lax.axis_index("seq").reshape(1)

    cache = (requests, key_cache.shape[1], size)
    packed, residual, gain = call(
        attention_kernel,
        (
            bf(requests, heads, 2 * size),
            bf(requests, width),
            jax.ShapeDtypeStruct((1, width), F32),
        ),
        12,
        scratch=[
            pltpu.SMEM((requests,), jnp.int32),
            pltpu.VMEM((requests, heads, size), BF),
            pltpu.VMEM((requests, size), BF),
            pltpu.VMEM(cache, BF),
            pltpu.VMEM((requests, size), BF),
            pltpu.VMEM(cache, BF),
            pltpu.VMEM((requests, width), BF),
            pltpu.VMEM((width // LANES, LANES), BF),
            DMA((8,)),
        ],
        smem=(0,),
        hbm=range(1, 12),
    )(
        where,
        lengths,
        queries,
        token_keys.reshape(requests, size),
        key_cache.reshape(cache),
        token_values.reshape(requests, size),
        cached_value_rows.reshape(cache),
        residual,
        norm_gain.reshape(-1, LANES),
        gate_weight,
        up_weight,
        down_weight,
    )
    got = exchange(packed.reshape(seq, rows, 2 * size), "seq")
    merged = call(merge_kernel, bf(seq, rows, size), 1)(got)
    attended, projected = call(
        project_kernel,
        (bf(requests, heads * size), bf(requests, width)),
        2,
        scratch=[pltpu.VMEM((requests * heads, size), F32)],
    )(exchange(merged, "seq"), out_weight)
    middle, pieces = call(
        gate_up_kernel,
        (bf(requests, width), bf(seq, depth, LANES)),
        5,
        scratch=[
            pltpu.VMEM((seq * depth, LANES), F32),
        ],
    )(parts_kvh(projected), residual, gain, gate_weight, up_weight)
    hidden = call(lambda *refs: hidden_kernel(blocks, *refs), bf(seq, thin, LANES), 1)(
        exchange(pieces, "seq")
    )
    down = call(
        down_kernel,
        bf(requests, width),
        2,
        scratch=[pltpu.VMEM((seq * thin, LANES), F32)],
    )(exchange(hidden, "seq"), down_weight)
    updated = call(finish_kernel, bf(requests, width), 2)(parts_kvh(down), middle)
    return (updated, attended)


def solution(mesh):
    return jax.shard_map(
        shards,
        mesh=mesh,
        in_specs=(
            P(None, "kvh", None),
            P(None, "kvh", None),
            P(None, "kvh", None),
            P(None, "seq", "kvh", None),
            P(None, "seq", "kvh", None),
            P(),
            P(None, "seq"),
            P("kvh", "seq"),
            P("seq"),
            P("seq", "kvh"),
            P("seq", "kvh"),
            P("kvh", "seq"),
        ),
        out_specs=(P(None, "seq"), P(None, "kvh")),
        check_vma=False,
    )
```

```python
import jax
import jax.numpy as jnp
from jax import lax
from jax.experimental import pallas as pl
from jax.experimental.pallas import tpu as pltpu
from jax.sharding import PartitionSpec as P

D = 16384
BF = jnp.bfloat16
F32 = jnp.float32
LANES = 128
MIB = 1 << 20
FAST = {"seq": 8, "kvh": 2}
VMEM = pl.BlockSpec(memory_space=pltpu.VMEM)
SMEM = pl.BlockSpec(memory_space=pltpu.SMEM)
HBM = pl.BlockSpec(memory_space=pltpu.HBM)
DMA = pltpu.SemaphoreType.DMA


def call(body, out_shape, n_in, scratch=(), smem=(), hbm=(), limit=16 * MIB):
    kernel = pl.pallas_call(
        body,
        out_shape=out_shape,
        in_specs=[SMEM if i in smem else HBM if i in hbm else VMEM for i in range(n_in)],
        out_specs=jax.tree.map(lambda _: VMEM, out_shape),
        scratch_shapes=list(scratch),
        compiler_params=pltpu.CompilerParams(vmem_limit_bytes=limit),
    )

    def run(*args):
        return kernel(
            *[
                pltpu.with_memory_space_constraint(arg, pltpu.HBM) if i in hbm else arg
                for i, arg in enumerate(args)
            ]
        )

    return run


def bf(*shape):
    return jax.ShapeDtypeStruct(shape, BF)


def round_bf(value):
    return value.astype(BF).astype(F32)


def lane_index(shape):
    return lax.broadcasted_iota(jnp.int32, shape, len(shape) - 1)


def stat_rows(columns):
    rows = columns[0].shape[0]
    lane = lane_index((rows, LANES))
    out = jnp.zeros((rows, LANES), F32)
    for index, column in enumerate(columns):
        out = jnp.where(lane == index, column, out)
    return out


def two_parts(value):
    high = round_bf(value)
    return high, value - high


def start_copies(sources, targets, sems):
    copies = [
        pltpu.make_async_copy(source, target, sems.at[i])
        for i, (source, target) in enumerate(zip(sources, targets))
    ]
    for copy in copies:
        copy.start()
    return copies


def attention_kernel(where_ref, *refs):
    sources, refs = refs[:8], refs[-12:]
    out_ref, kept_ref, row_ref = refs[:3]
    targets, sems = refs[3:11], refs[11]
    len_ref, q_ref, tk_ref, k_ref, tv_ref, v_ref, res_ref, gn_ref = targets
    copies = start_copies(sources, targets, sems)
    for copy in copies[:4]:
        copy.wait()
    requests, heads, size = q_ref.shape
    slots = k_ref.shape[1]
    scale = size ** (-0.5)
    first = where_ref[0] * slots
    owner = where_ref[0] == 0
    contract = (((1,), (1,)), ((), ()))
    slot = first + lane_index((heads, slots))
    scores, valid, fresh = [], [], []
    for b in range(requests):
        q = q_ref[b]
        scores.append(lax.dot_general(q, k_ref[b], contract, preferred_element_type=F32))
        valid.append(jnp.where(slot < len_ref[b], 1.0, 0.0))
        fresh.append(q.astype(F32) * tk_ref[b : b + 1, :].astype(F32))
    valid = jnp.concatenate(valid, 0) > 0.5
    scores = jnp.where(valid, jnp.concatenate(scores, 0) * scale, -1e30)
    fresh = jnp.sum(jnp.concatenate(fresh, 0), -1, keepdims=True) * scale
    fresh = jnp.where(owner, fresh, -1e30)
    peak = round_bf(jnp.maximum(jnp.max(scores, -1, keepdims=True), fresh))
    weights = jnp.where(valid, jnp.exp(scores - peak), 0.0)
    own = jnp.where(owner, jnp.exp(fresh - peak), 0.0)
    total = jnp.sum(weights, -1, keepdims=True) + own
    rounded = weights.astype(BF)
    own = round_bf(own)
    stats = stat_rows((peak,) + two_parts(total)).astype(BF)
    for copy in copies[4:]:
        copy.wait()
    for b in range(requests):
        rows = slice(b * heads, (b + 1) * heads)
        acc = jnp.dot(rounded[rows], v_ref[b], preferred_element_type=F32)
        acc = acc + own[rows] * tv_ref[b : b + 1, :].astype(F32)
        out_ref[b, :, :size] = acc.astype(BF)
        out_ref[b, :, size:] = stats[rows]
    kept_ref[...] = res_ref[...]
    gain = gn_ref[...].astype(F32)
    row_ref[...] = jnp.concatenate([gain[i : i + 1] for i in range(gain.shape[0])], -1)


def merge_kernel(got_ref, out_ref):
    size = out_ref.shape[-1]
    stats = got_ref[:, :, size:].astype(F32)
    peak = stats[:, :, 0:1]
    factor = jnp.exp(peak - jnp.max(peak, 0, keepdims=True))
    total = jnp.sum((stats[:, :, 1:2] + stats[:, :, 2:3]) * factor, 0)
    acc = jnp.sum(got_ref[:, :, :size].astype(F32) * factor, 0)
    out_ref[...] = jnp.broadcast_to((acc / total).astype(BF)[None], out_ref.shape)


def project_kernel(got_ref, weight_ref, attended_ref, out_ref, rows_ref):
    requests = attended_ref.shape[0]
    heads = rows_ref.shape[0] // requests
    rows_ref[...] = got_ref[...].astype(F32).reshape(rows_ref.shape)
    attended = jnp.concatenate(
        [rows_ref[pl.ds(h, requests, stride=heads), :].astype(BF) for h in range(heads)], -1
    )
    attended_ref[...] = attended
    projected = jnp.dot(attended, weight_ref[...], preferred_element_type=F32)
    out_ref[...] = jnp.broadcast_to(projected.astype(BF)[None], out_ref.shape)


def gate_up_kernel(
    got_ref, residual_ref, gain_ref, gate_ref, up_ref, middle_ref, out_ref, rows_ref
):
    pieces, depth, _ = out_ref.shape
    requests = residual_ref.shape[0]
    halves = pieces // requests
    projected = jnp.sum(got_ref[...].astype(F32), 0)
    middle = (residual_ref[...].astype(F32) + projected).astype(BF)
    middle_ref[...] = middle
    middle = middle.astype(F32)
    square = jnp.sum(middle * middle, -1, keepdims=True)
    scaled = (middle * gain_ref[...]).astype(BF)
    blocks = gate_ref.shape[1] // (halves * LANES)

    def put(row, half, value):
        rows_ref[pl.ds(half * depth + row, requests, stride=halves * depth), :] = value

    for start, weight_ref in ((0, gate_ref), (blocks, up_ref)):
        product = jnp.dot(scaled, weight_ref[...], preferred_element_type=F32)
        for j in range(halves * blocks):
            put(start + j % blocks, j // blocks, product[:, j * LANES : (j + 1) * LANES])
    stats = stat_rows(two_parts(square))
    zeros = jnp.zeros_like(stats)
    for half in range(halves):
        put(2 * blocks, half, stats)
        for row in range(2 * blocks + 1, depth):
            put(row, half, zeros)
    out_ref[...] = rows_ref[...].astype(BF).reshape(out_ref.shape)


def hidden_kernel(blocks, got_ref, out_ref):
    summed = jnp.sum(got_ref[...].astype(F32), 0)
    stats = summed[2 * blocks : 2 * blocks + 1]
    square = stats[:, 0:1] + stats[:, 1:2]
    inverse = lax.rsqrt(square / D + 1e-05)
    gate = summed[:blocks] * inverse
    up = summed[blocks : 2 * blocks] * inverse
    hidden = gate / (1.0 + jnp.exp(-gate)) * up
    pad = jnp.zeros((out_ref.shape[1] - blocks, LANES), F32)
    hidden = jnp.concatenate([hidden, pad], 0).astype(BF)
    out_ref[...] = jnp.broadcast_to(hidden[None], out_ref.shape)


def down_kernel(got_ref, weight_ref, out_ref, rows_ref):
    pieces, depth, _ = got_ref.shape
    requests = out_ref.shape[1]
    halves = pieces // requests
    blocks = weight_ref.shape[0] // (halves * LANES)
    rows_ref[...] = got_ref[...].astype(F32).reshape(rows_ref.shape)
    hidden = jnp.concatenate(
        [
            rows_ref[pl.ds(half * depth + row, requests, stride=halves * depth), :].astype(BF)
            for half in range(halves)
            for row in range(blocks)
        ],
        -1,
    )
    down = jnp.dot(hidden, weight_ref[...], preferred_element_type=F32)
    out_ref[...] = jnp.broadcast_to(down.astype(BF)[None], out_ref.shape)


def finish_kernel(got_ref, middle_ref, out_ref):
    down = jnp.sum(got_ref[...].astype(F32), 0)
    out_ref[...] = (middle_ref[...].astype(F32) + down).astype(BF)


def exchange(pieces, axis):
    size, fast = lax.axis_size(axis), FAST[axis]
    order = [slow * fast + last for last in range(fast) for slow in range(size // fast)]
    return lax.all_to_all(pieces, axis, 0, 0, axis_index_groups=[order])


def shards(
    queries,
    token_keys,
    token_values,
    key_cache,
    cached_value_rows,
    lengths,
    residual,
    out_weight,
    norm_gain,
    gate_weight,
    up_weight,
    down_weight,
):
    requests, heads, size = queries.shape
    seq, kvh = lax.axis_size("seq"), lax.axis_size("kvh")
    rows = requests * heads // seq
    width = residual.shape[1]
    halves = seq // requests
    blocks = gate_weight.shape[1] // (halves * LANES)
    depth = -(-(2 * blocks + 1) // 16) * 16
    thin = -(-blocks // 16) * 16
    where = lax.axis_index("seq").reshape(1)

    cache = (requests, key_cache.shape[1], size)
    packed, residual, gain = call(
        attention_kernel,
        (
            bf(requests, heads, 2 * size),
            bf(requests, width),
            jax.ShapeDtypeStruct((1, width), F32),
        ),
        12,
        scratch=[
            pltpu.SMEM((requests,), jnp.int32),
            pltpu.VMEM((requests, heads, size), BF),
            pltpu.VMEM((requests, size), BF),
            pltpu.VMEM(cache, BF),
            pltpu.VMEM((requests, size), BF),
            pltpu.VMEM(cache, BF),
            pltpu.VMEM((requests, width), BF),
            pltpu.VMEM((width // LANES, LANES), BF),
            DMA((8,)),
        ],
        smem=(0,),
        hbm=range(1, 12),
    )(
        where,
        lengths,
        queries,
        token_keys.reshape(requests, size),
        key_cache.reshape(cache),
        token_values.reshape(requests, size),
        cached_value_rows.reshape(cache),
        residual,
        norm_gain.reshape(-1, LANES),
        gate_weight,
        up_weight,
        down_weight,
    )
    got = exchange(packed.reshape(seq, rows, 2 * size), "seq")
    merged = call(merge_kernel, bf(seq, rows, size), 1)(got)
    attended, projected = call(
        project_kernel,
        (bf(requests, heads * size), bf(kvh, requests, width)),
        2,
        scratch=[pltpu.VMEM((requests * heads, size), F32)],
    )(exchange(merged, "seq"), out_weight)
    middle, pieces = call(
        gate_up_kernel,
        (bf(requests, width), bf(seq, depth, LANES)),
        5,
        scratch=[
            pltpu.VMEM((seq * depth, LANES), F32),
        ],
    )(exchange(projected, "kvh"), residual, gain, gate_weight, up_weight)
    hidden = call(lambda *refs: hidden_kernel(blocks, *refs), bf(seq, thin, LANES), 1)(
        exchange(pieces, "seq")
    )
    down = call(
        down_kernel,
        bf(kvh, requests, width),
        2,
        scratch=[pltpu.VMEM((seq * thin, LANES), F32)],
    )(exchange(hidden, "seq"), down_weight)
    updated = call(finish_kernel, bf(requests, width), 2)(exchange(down, "kvh"), middle)
    return (updated, attended)


def solution(mesh):
    return jax.shard_map(
        shards,
        mesh=mesh,
        in_specs=(
            P(None, "kvh", None),
            P(None, "kvh", None),
            P(None, "kvh", None),
            P(None, "seq", "kvh", None),
            P(None, "seq", "kvh", None),
            P(),
            P(None, "seq"),
            P("kvh", "seq"),
            P("seq"),
            P("seq", "kvh"),
            P("seq", "kvh"),
            P("kvh", "seq"),
        ),
        out_specs=(P(None, "seq"), P(None, "kvh")),
        check_vma=False,
    )
```

```python
import jax
import jax.numpy as jnp
from jax import lax
from jax.experimental import pallas as pl
from jax.experimental.pallas import tpu as pltpu
from jax.sharding import PartitionSpec as P

D = 16384
BF = jnp.bfloat16
F32 = jnp.float32
LANES = 128
MIB = 1 << 20
CORES = 2
VMEM = pl.BlockSpec(memory_space=pltpu.VMEM)
SMEM = pl.BlockSpec(memory_space=pltpu.SMEM)
HBM = pl.BlockSpec(memory_space=pltpu.HBM)
DMA = pltpu.SemaphoreType.DMA


def call(body, out_shape, n_in, scratch=(), smem=(), hbm=(), hbm_out=(), limit=16 * MIB):
    kernel = pl.pallas_call(
        body,
        out_shape=out_shape,
        in_specs=[SMEM if i in smem else HBM if i in hbm else VMEM for i in range(n_in)],
        out_specs=tuple(HBM if i in hbm_out else VMEM for i in range(len(out_shape)))
        if isinstance(out_shape, tuple)
        else VMEM,
        scratch_shapes=list(scratch),
        compiler_params=pltpu.CompilerParams(vmem_limit_bytes=limit),
    )

    def run(*args):
        return kernel(
            *[
                pltpu.with_memory_space_constraint(arg, pltpu.HBM) if i in hbm else arg
                for i, arg in enumerate(args)
            ]
        )

    return run


def bf(*shape):
    return jax.ShapeDtypeStruct(shape, BF)


def round_bf(value):
    return value.astype(BF).astype(F32)


def lane_index(shape):
    return lax.broadcasted_iota(jnp.int32, shape, len(shape) - 1)


def stat_rows(columns):
    rows = columns[0].shape[0]
    lane = lane_index((rows, LANES))
    out = jnp.zeros((rows, LANES), F32)
    for index, column in enumerate(columns):
        out = jnp.where(lane == index, column, out)
    return out


def two_parts(value):
    high = round_bf(value)
    return high, value - high


def start_copies(sources, targets, sems):
    copies = [
        pltpu.make_async_copy(source, target, sems.at[i])
        for i, (source, target) in enumerate(zip(sources, targets))
    ]
    for copy in copies:
        copy.start()
    return copies


def attention_kernel(where_ref, *refs):
    sources, refs = refs[:8], refs[-12:]
    out_ref, kept_ref, row_ref = refs[:3]
    targets, sems = refs[3:11], refs[11]
    len_ref, q_ref, tk_ref, k_ref, tv_ref, v_ref, res_ref, gn_ref = targets
    copies = start_copies(sources, targets, sems)
    for copy in copies[:4]:
        copy.wait()
    requests, heads, size = q_ref.shape
    slots = k_ref.shape[1]
    scale = size ** (-0.5)
    first = where_ref[0] * slots
    owner = where_ref[0] == 0
    contract = (((1,), (1,)), ((), ()))
    slot = first + lane_index((heads, slots))
    scores, valid, fresh = [], [], []
    for b in range(requests):
        q = q_ref[b]
        scores.append(lax.dot_general(q, k_ref[b], contract, preferred_element_type=F32))
        valid.append(jnp.where(slot < len_ref[b], 1.0, 0.0))
        fresh.append(q.astype(F32) * tk_ref[b : b + 1, :].astype(F32))
    valid = jnp.concatenate(valid, 0) > 0.5
    scores = jnp.where(valid, jnp.concatenate(scores, 0) * scale, -1e30)
    fresh = jnp.sum(jnp.concatenate(fresh, 0), -1, keepdims=True) * scale
    fresh = jnp.where(owner, fresh, -1e30)
    peak = round_bf(jnp.maximum(jnp.max(scores, -1, keepdims=True), fresh))
    weights = jnp.where(valid, jnp.exp(scores - peak), 0.0)
    own = jnp.where(owner, jnp.exp(fresh - peak), 0.0)
    total = jnp.sum(weights, -1, keepdims=True) + own
    rounded = weights.astype(BF)
    own = round_bf(own)
    stats = stat_rows((peak,) + two_parts(total)).astype(BF)
    for copy in copies[4:]:
        copy.wait()
    for b in range(requests):
        rows = slice(b * heads, (b + 1) * heads)
        acc = jnp.dot(rounded[rows], v_ref[b], preferred_element_type=F32)
        acc = acc + own[rows] * tv_ref[b : b + 1, :].astype(F32)
        out_ref[b, :, :size] = acc.astype(BF)
        out_ref[b, :, size:] = stats[rows]
    kept_ref[...] = res_ref[...]
    gain = gn_ref[...].astype(F32)
    row_ref[...] = jnp.concatenate([gain[i : i + 1] for i in range(gain.shape[0])], -1)


def merge_kernel(got_ref, out_ref):
    size = out_ref.shape[-1]
    stats = got_ref[:, :, size:].astype(F32)
    peak = stats[:, :, 0:1]
    factor = jnp.exp(peak - jnp.max(peak, 0, keepdims=True))
    total = jnp.sum((stats[:, :, 1:2] + stats[:, :, 2:3]) * factor, 0)
    acc = jnp.sum(got_ref[:, :, :size].astype(F32) * factor, 0)
    out_ref[...] = jnp.broadcast_to((acc / total).astype(BF)[None], out_ref.shape)


def project_kernel(got_ref, weight_ref, attended_ref, out_ref, rows_ref):
    requests = attended_ref.shape[0]
    heads = rows_ref.shape[0] // requests
    rows_ref[...] = got_ref[...].astype(F32).reshape(rows_ref.shape)
    attended = jnp.concatenate(
        [rows_ref[pl.ds(h, requests, stride=heads), :].astype(BF) for h in range(heads)], -1
    )
    attended_ref[...] = attended
    projected = jnp.dot(attended, weight_ref[...], preferred_element_type=F32)
    out_ref[...] = jnp.broadcast_to(projected.astype(BF)[None], out_ref.shape)


def gate_up_kernel(
    got_ref, residual_ref, gain_ref, gate_ref, up_ref, attended_ref,
    middle_ref, out_ref, result_ref, rows_ref, sems,
):
    writes = start_copies([attended_ref], [result_ref], sems)
    pieces, depth, _ = out_ref.shape
    requests = residual_ref.shape[0]
    halves = pieces // requests
    projected = jnp.sum(got_ref[...].astype(F32), 0)
    middle = (residual_ref[...].astype(F32) + projected).astype(BF)
    middle_ref[...] = middle
    middle = middle.astype(F32)
    square = jnp.sum(middle * middle, -1, keepdims=True)
    scaled = (middle * gain_ref[...]).astype(BF)
    blocks = gate_ref.shape[1] // (halves * LANES)

    def put(row, half, value):
        rows_ref[pl.ds(half * depth + row, requests, stride=halves * depth), :] = value

    for start, weight_ref in ((0, gate_ref), (blocks, up_ref)):
        product = jnp.dot(scaled, weight_ref[...], preferred_element_type=F32)
        for j in range(halves * blocks):
            put(start + j % blocks, j // blocks, product[:, j * LANES : (j + 1) * LANES])
    stats = stat_rows(two_parts(square))
    zeros = jnp.zeros_like(stats)
    for half in range(halves):
        put(2 * blocks, half, stats)
        for row in range(2 * blocks + 1, depth):
            put(row, half, zeros)
    out_ref[...] = rows_ref[...].astype(BF).reshape(out_ref.shape)
    for write in writes:
        write.wait()


def hidden_kernel(blocks, got_ref, out_ref):
    summed = jnp.sum(got_ref[...].astype(F32), 0)
    stats = summed[2 * blocks : 2 * blocks + 1]
    square = stats[:, 0:1] + stats[:, 1:2]
    inverse = lax.rsqrt(square / D + 1e-05)
    gate = summed[:blocks] * inverse
    up = summed[blocks : 2 * blocks] * inverse
    hidden = gate / (1.0 + jnp.exp(-gate)) * up
    pad = jnp.zeros((out_ref.shape[1] - blocks, LANES), F32)
    hidden = jnp.concatenate([hidden, pad], 0).astype(BF)
    out_ref[...] = jnp.broadcast_to(hidden[None], out_ref.shape)


def down_kernel(got_ref, weight_ref, out_ref, rows_ref):
    pieces, depth, _ = got_ref.shape
    requests = out_ref.shape[1]
    halves = pieces // requests
    blocks = weight_ref.shape[0] // (halves * LANES)
    rows_ref[...] = got_ref[...].astype(F32).reshape(rows_ref.shape)
    hidden = jnp.concatenate(
        [
            rows_ref[pl.ds(half * depth + row, requests, stride=halves * depth), :].astype(BF)
            for half in range(halves)
            for row in range(blocks)
        ],
        -1,
    )
    down = jnp.dot(hidden, weight_ref[...], preferred_element_type=F32)
    out_ref[...] = jnp.broadcast_to(down.astype(BF)[None], out_ref.shape)


def finish_kernel(got_ref, middle_ref, out_ref):
    down = jnp.sum(got_ref[...].astype(F32), 0)
    out_ref[...] = (middle_ref[...].astype(F32) + down).astype(BF)


def exchange(pieces, axis):
    return lax.all_to_all(pieces, axis, 0, 0)


def parts_kvh(pieces):
    size = lax.axis_size("kvh")
    order = [chip * CORES + core for core in range(CORES) for chip in range(size // CORES)]
    return lax.all_to_all(pieces, "kvh", 0, 0, axis_index_groups=[order])


def shards(
    queries,
    token_keys,
    token_values,
    key_cache,
    cached_value_rows,
    lengths,
    residual,
    out_weight,
    norm_gain,
    gate_weight,
    up_weight,
    down_weight,
):
    requests, heads, size = queries.shape
    seq, kvh = lax.axis_size("seq"), lax.axis_size("kvh")
    rows = requests * heads // seq
    width = residual.shape[1]
    halves = seq // requests
    blocks = gate_weight.shape[1] // (halves * LANES)
    depth = -(-(2 * blocks + 1) // 16) * 16
    thin = -(-blocks // 16) * 16
    where = lax.axis_index("seq").reshape(1)

    cache = (requests, key_cache.shape[1], size)
    packed, residual, gain = call(
        attention_kernel,
        (
            bf(requests, heads, 2 * size),
            bf(requests, width),
            jax.ShapeDtypeStruct((1, width), F32),
        ),
        12,
        scratch=[
            pltpu.SMEM((requests,), jnp.int32),
            pltpu.VMEM((requests, heads, size), BF),
            pltpu.VMEM((requests, size), BF),
            pltpu.VMEM(cache, BF),
            pltpu.VMEM((requests, size), BF),
            pltpu.VMEM(cache, BF),
            pltpu.VMEM((requests, width), BF),
            pltpu.VMEM((width // LANES, LANES), BF),
            DMA((8,)),
        ],
        smem=(0,),
        hbm=range(1, 12),
    )(
        where,
        lengths,
        queries,
        token_keys.reshape(requests, size),
        key_cache.reshape(cache),
        token_values.reshape(requests, size),
        cached_value_rows.reshape(cache),
        residual,
        norm_gain.reshape(-1, LANES),
        gate_weight,
        up_weight,
        down_weight,
    )
    got = exchange(packed.reshape(seq, rows, 2 * size), "seq")
    merged = call(merge_kernel, bf(seq, rows, size), 1)(got)
    attended, projected = call(
        project_kernel,
        (bf(requests, heads * size), bf(kvh, requests, width)),
        2,
        scratch=[pltpu.VMEM((requests * heads, size), F32)],
    )(exchange(merged, "seq"), out_weight)
    middle, pieces, attended = call(
        gate_up_kernel,
        (bf(requests, width), bf(seq, depth, LANES), bf(requests, heads * size)),
        6,
        scratch=[pltpu.VMEM((seq * depth, LANES), F32), DMA((1,))],
        hbm_out=(2,),
    )(parts_kvh(projected), residual, gain, gate_weight, up_weight, attended)
    hidden = call(lambda *refs: hidden_kernel(blocks, *refs), bf(seq, thin, LANES), 1)(
        exchange(pieces, "seq")
    )
    down = call(
        down_kernel,
        bf(kvh, requests, width),
        2,
        scratch=[pltpu.VMEM((seq * thin, LANES), F32)],
    )(exchange(hidden, "seq"), down_weight)
    updated = call(finish_kernel, bf(requests, width), 2)(parts_kvh(down), middle)
    return (updated, attended)


def solution(mesh):
    return jax.shard_map(
        shards,
        mesh=mesh,
        in_specs=(
            P(None, "kvh", None),
            P(None, "kvh", None),
            P(None, "kvh", None),
            P(None, "seq", "kvh", None),
            P(None, "seq", "kvh", None),
            P(),
            P(None, "seq"),
            P("kvh", "seq"),
            P("seq"),
            P("seq", "kvh"),
            P("seq", "kvh"),
            P("kvh", "seq"),
        ),
        out_specs=(P(None, "seq"), P(None, "kvh")),
        check_vma=False,
    )
```

```python
import jax
import jax.numpy as jnp
from jax import lax
from jax.experimental import pallas as pl
from jax.experimental.pallas import tpu as pltpu
from jax.sharding import PartitionSpec as P

D = 16384
BF = jnp.bfloat16
F32 = jnp.float32
LANES = 128
MIB = 1 << 20
CORES = 2
VMEM = pl.BlockSpec(memory_space=pltpu.VMEM)
SMEM = pl.BlockSpec(memory_space=pltpu.SMEM)
HBM = pl.BlockSpec(memory_space=pltpu.HBM)
DMA = pltpu.SemaphoreType.DMA


def call(body, out_shape, n_in, scratch=(), smem=(), hbm=(), hbm_out=(), limit=16 * MIB):
    kernel = pl.pallas_call(
        body,
        out_shape=out_shape,
        in_specs=[SMEM if i in smem else HBM if i in hbm else VMEM for i in range(n_in)],
        out_specs=tuple(HBM if i in hbm_out else VMEM for i in range(len(out_shape)))
        if isinstance(out_shape, tuple)
        else VMEM,
        scratch_shapes=list(scratch),
        compiler_params=pltpu.CompilerParams(vmem_limit_bytes=limit),
    )

    def run(*args):
        return kernel(
            *[
                pltpu.with_memory_space_constraint(arg, pltpu.HBM) if i in hbm else arg
                for i, arg in enumerate(args)
            ]
        )

    return run


def bf(*shape):
    return jax.ShapeDtypeStruct(shape, BF)


def round_bf(value):
    return value.astype(BF).astype(F32)


def lane_index(shape):
    return lax.broadcasted_iota(jnp.int32, shape, len(shape) - 1)


def stat_rows(columns):
    rows = columns[0].shape[0]
    lane = lane_index((rows, LANES))
    out = jnp.zeros((rows, LANES), F32)
    for index, column in enumerate(columns):
        out = jnp.where(lane == index, column, out)
    return out


def two_parts(value):
    high = round_bf(value)
    return high, value - high


def start_copies(sources, targets, sems):
    copies = [
        pltpu.make_async_copy(source, target, sems.at[i])
        for i, (source, target) in enumerate(zip(sources, targets))
    ]
    for copy in copies:
        copy.start()
    return copies


def attention_kernel(where_ref, *refs):
    sources, refs = refs[:8], refs[-12:]
    out_ref, kept_ref, row_ref = refs[:3]
    targets, sems = refs[3:11], refs[11]
    len_ref, q_ref, tk_ref, k_ref, tv_ref, v_ref, res_ref, gn_ref = targets
    requests, heads, size = q_ref.shape
    halves = [pl.ds(i * requests // 2, requests // 2) for i in range(2)]
    large = [i for i in range(len(targets)) if targets[i] is k_ref or targets[i] is v_ref]
    small = [i for i in range(len(targets)) if i not in large]
    pairs = [(sources[i].at[h], targets[i].at[h]) for i in large for h in halves]
    pairs += [(sources[i], targets[i]) for i in small]
    copies = start_copies(*zip(*pairs), sems)
    keys, values, others = copies[:2], copies[2:4], copies[4:]
    for copy in keys + others:
        copy.wait()
    slots = k_ref.shape[1]
    scale = size ** (-0.5)
    first = where_ref[0] * slots
    owner = where_ref[0] == 0
    contract = (((1,), (1,)), ((), ()))
    slot = first + lane_index((heads, slots))
    scores, valid, fresh = [], [], []
    for b in range(requests):
        q = q_ref[b]
        scores.append(lax.dot_general(q, k_ref[b], contract, preferred_element_type=F32))
        valid.append(jnp.where(slot < len_ref[b], 1.0, 0.0))
        fresh.append(q.astype(F32) * tk_ref[b : b + 1, :].astype(F32))
    valid = jnp.concatenate(valid, 0) > 0.5
    scores = jnp.where(valid, jnp.concatenate(scores, 0) * scale, -1e30)
    fresh = jnp.sum(jnp.concatenate(fresh, 0), -1, keepdims=True) * scale
    fresh = jnp.where(owner, fresh, -1e30)
    peak = round_bf(jnp.maximum(jnp.max(scores, -1, keepdims=True), fresh))
    weights = jnp.where(valid, jnp.exp(scores - peak), 0.0)
    own = jnp.where(owner, jnp.exp(fresh - peak), 0.0)
    total = jnp.sum(weights, -1, keepdims=True) + own
    rounded = weights.astype(BF)
    own = round_bf(own)
    stats = stat_rows((peak,) + two_parts(total)).astype(BF)
    for copy in values:
        copy.wait()
    for b in range(requests):
        rows = slice(b * heads, (b + 1) * heads)
        acc = jnp.dot(rounded[rows], v_ref[b], preferred_element_type=F32)
        acc = acc + own[rows] * tv_ref[b : b + 1, :].astype(F32)
        out_ref[b, :, :size] = acc.astype(BF)
        out_ref[b, :, size:] = stats[rows]
    kept_ref[...] = res_ref[...]
    gain = gn_ref[...].astype(F32)
    row_ref[...] = jnp.concatenate([gain[i : i + 1] for i in range(gain.shape[0])], -1)


def merge_kernel(got_ref, out_ref):
    size = out_ref.shape[-1]
    stats = got_ref[:, :, size:].astype(F32)
    peak = stats[:, :, 0:1]
    factor = jnp.exp(peak - jnp.max(peak, 0, keepdims=True))
    total = jnp.sum((stats[:, :, 1:2] + stats[:, :, 2:3]) * factor, 0)
    acc = jnp.sum(got_ref[:, :, :size].astype(F32) * factor, 0)
    out_ref[...] = jnp.broadcast_to((acc / total).astype(BF)[None], out_ref.shape)


def project_kernel(got_ref, weight_ref, attended_ref, out_ref, rows_ref):
    requests = attended_ref.shape[0]
    heads = rows_ref.shape[0] // requests
    rows_ref[...] = got_ref[...].astype(F32).reshape(rows_ref.shape)
    attended = jnp.concatenate(
        [rows_ref[pl.ds(h, requests, stride=heads), :].astype(BF) for h in range(heads)], -1
    )
    attended_ref[...] = attended
    projected = jnp.dot(attended, weight_ref[...], preferred_element_type=F32)
    out_ref[...] = projected.astype(BF)


def gate_up_kernel(
    where_ref, p0_ref, p1_ref, p2_ref, p3_ref, residual_ref, gain_ref, gate_ref, up_ref,
    attended_ref, middle_ref, out_ref, result_ref, rows_ref, slots_ref, sems,
):
    writes = start_copies([attended_ref], [result_ref], sems)
    pieces, depth, _ = out_ref.shape
    requests = residual_ref.shape[0]
    halves = pieces // requests
    projected = sum_in_order(where_ref, (p0_ref, p1_ref, p2_ref, p3_ref), slots_ref)
    middle = (residual_ref[...].astype(F32) + projected).astype(BF)
    middle_ref[...] = middle
    middle = middle.astype(F32)
    square = jnp.sum(middle * middle, -1, keepdims=True)
    scaled = (middle * gain_ref[...]).astype(BF)
    blocks = gate_ref.shape[1] // (halves * LANES)

    def put(row, half, value):
        rows_ref[pl.ds(half * depth + row, requests, stride=halves * depth), :] = value

    for start, weight_ref in ((0, gate_ref), (blocks, up_ref)):
        product = jnp.dot(scaled, weight_ref[...], preferred_element_type=F32)
        for j in range(halves * blocks):
            put(start + j % blocks, j // blocks, product[:, j * LANES : (j + 1) * LANES])
    stats = stat_rows(two_parts(square))
    zeros = jnp.zeros_like(stats)
    for half in range(halves):
        put(2 * blocks, half, stats)
        for row in range(2 * blocks + 1, depth):
            put(row, half, zeros)
    out_ref[...] = rows_ref[...].astype(BF).reshape(out_ref.shape)
    for write in writes:
        write.wait()


def hidden_kernel(blocks, got_ref, out_ref):
    summed = jnp.sum(got_ref[...].astype(F32), 0)
    stats = summed[2 * blocks : 2 * blocks + 1]
    square = stats[:, 0:1] + stats[:, 1:2]
    inverse = lax.rsqrt(square / D + 1e-05)
    gate = summed[:blocks] * inverse
    up = summed[blocks : 2 * blocks] * inverse
    hidden = gate / (1.0 + jnp.exp(-gate)) * up
    pad = jnp.zeros((out_ref.shape[1] - blocks, LANES), F32)
    hidden = jnp.concatenate([hidden, pad], 0).astype(BF)
    out_ref[...] = jnp.broadcast_to(hidden[None], out_ref.shape)


def down_kernel(got_ref, weight_ref, out_ref, rows_ref):
    pieces, depth, _ = got_ref.shape
    requests = out_ref.shape[0]
    halves = pieces // requests
    blocks = weight_ref.shape[0] // (halves * LANES)
    rows_ref[...] = got_ref[...].astype(F32).reshape(rows_ref.shape)
    hidden = jnp.concatenate(
        [
            rows_ref[pl.ds(half * depth + row, requests, stride=halves * depth), :].astype(BF)
            for half in range(halves)
            for row in range(blocks)
        ],
        -1,
    )
    down = jnp.dot(hidden, weight_ref[...], preferred_element_type=F32)
    out_ref[...] = down.astype(BF)


def finish_kernel(where_ref, p0_ref, p1_ref, p2_ref, p3_ref, middle_ref, out_ref, slots_ref):
    down = sum_in_order(where_ref, (p0_ref, p1_ref, p2_ref, p3_ref), slots_ref)
    out_ref[...] = (middle_ref[...].astype(F32) + down).astype(BF)


def add_kernel(a_ref, b_ref, out_ref):
    out_ref[...] = (a_ref[...].astype(F32) + b_ref[...].astype(F32)).astype(BF)


def sum_in_order(where_ref, refs, slots_ref):
    own = where_ref[0] // CORES
    for k, ref in enumerate(refs):
        slots_ref[own ^ k] = ref[...].astype(F32)
    return jnp.sum(slots_ref[...], 0)


def exchange(pieces, axis):
    return lax.all_to_all(pieces, axis, 0, 0)


def swap(value, mask):
    pairs = [(i, i ^ mask) for i in range(lax.axis_size("kvh"))]
    return lax.ppermute(value, "kvh", pairs)


def parts_kvh(value):
    both = call(add_kernel, bf(*value.shape), 2)(value, swap(value, 1))
    return [both] + [swap(both, k * CORES) for k in (1, 2, 3)]


def shards(
    queries,
    token_keys,
    token_values,
    key_cache,
    cached_value_rows,
    lengths,
    residual,
    out_weight,
    norm_gain,
    gate_weight,
    up_weight,
    down_weight,
):
    requests, heads, size = queries.shape
    seq = lax.axis_size("seq")
    group = lax.axis_index("kvh").reshape(1)
    rows = requests * heads // seq
    width = residual.shape[1]
    halves = seq // requests
    blocks = gate_weight.shape[1] // (halves * LANES)
    depth = -(-(2 * blocks + 1) // 16) * 16
    thin = -(-blocks // 16) * 16
    where = lax.axis_index("seq").reshape(1)

    cache = (requests, key_cache.shape[1], size)
    packed, residual, gain = call(
        attention_kernel,
        (
            bf(requests, heads, 2 * size),
            bf(requests, width),
            jax.ShapeDtypeStruct((1, width), F32),
        ),
        12,
        scratch=[
            pltpu.SMEM((requests,), jnp.int32),
            pltpu.VMEM((requests, heads, size), BF),
            pltpu.VMEM((requests, size), BF),
            pltpu.VMEM(cache, BF),
            pltpu.VMEM((requests, size), BF),
            pltpu.VMEM(cache, BF),
            pltpu.VMEM((requests, width), BF),
            pltpu.VMEM((width // LANES, LANES), BF),
            DMA((10,)),
        ],
        smem=(0,),
        hbm=range(1, 12),
    )(
        where,
        lengths,
        queries,
        token_keys.reshape(requests, size),
        key_cache.reshape(cache),
        token_values.reshape(requests, size),
        cached_value_rows.reshape(cache),
        residual,
        norm_gain.reshape(-1, LANES),
        gate_weight,
        up_weight,
        down_weight,
    )
    got = exchange(packed.reshape(seq, rows, 2 * size), "seq")
    merged = call(merge_kernel, bf(seq, rows, size), 1)(got)
    attended, projected = call(
        project_kernel,
        (bf(requests, heads * size), bf(requests, width)),
        2,
        scratch=[pltpu.VMEM((requests * heads, size), F32)],
    )(exchange(merged, "seq"), out_weight)
    middle, pieces, attended = call(
        gate_up_kernel,
        (bf(requests, width), bf(seq, depth, LANES), bf(requests, heads * size)),
        10,
        scratch=[
            pltpu.VMEM((seq * depth, LANES), F32),
            pltpu.VMEM((4, requests, width), F32),
            DMA((1,)),
        ],
        smem=(0,),
        hbm_out=(2,),
    )(group, *parts_kvh(projected), residual, gain, gate_weight, up_weight, attended)
    hidden = call(lambda *refs: hidden_kernel(blocks, *refs), bf(seq, thin, LANES), 1)(
        exchange(pieces, "seq")
    )
    down = call(
        down_kernel,
        bf(requests, width),
        2,
        scratch=[pltpu.VMEM((seq * thin, LANES), F32)],
    )(exchange(hidden, "seq"), down_weight)
    updated = call(
        finish_kernel,
        bf(requests, width),
        6,
        scratch=[pltpu.VMEM((4, requests, width), F32)],
        smem=(0,),
    )(group, *parts_kvh(down), middle)
    return (updated, attended)


def solution(mesh):
    return jax.shard_map(
        shards,
        mesh=mesh,
        in_specs=(
            P(None, "kvh", None),
            P(None, "kvh", None),
            P(None, "kvh", None),
            P(None, "seq", "kvh", None),
            P(None, "seq", "kvh", None),
            P(),
            P(None, "seq"),
            P("kvh", "seq"),
            P("seq"),
            P("seq", "kvh"),
            P("seq", "kvh"),
            P("kvh", "seq"),
        ),
        out_specs=(P(None, "seq"), P(None, "kvh")),
        check_vma=False,
    )
```

```python
import jax
import jax.numpy as jnp
from jax import lax
from jax.experimental import pallas as pl
from jax.experimental.pallas import tpu as pltpu
from jax.sharding import PartitionSpec as P

D = 16384
BF = jnp.bfloat16
F32 = jnp.float32
LANES = 128
MIB = 1 << 20
CORES = 2
VMEM = pl.BlockSpec(memory_space=pltpu.VMEM)
SMEM = pl.BlockSpec(memory_space=pltpu.SMEM)
HBM = pl.BlockSpec(memory_space=pltpu.HBM)
DMA = pltpu.SemaphoreType.DMA


def call(body, out_shape, n_in, scratch=(), smem=(), hbm=(), hbm_out=(), limit=16 * MIB):
    kernel = pl.pallas_call(
        body,
        out_shape=out_shape,
        in_specs=[SMEM if i in smem else HBM if i in hbm else VMEM for i in range(n_in)],
        out_specs=tuple(HBM if i in hbm_out else VMEM for i in range(len(out_shape)))
        if isinstance(out_shape, tuple)
        else VMEM,
        scratch_shapes=list(scratch),
        compiler_params=pltpu.CompilerParams(vmem_limit_bytes=limit),
    )

    def run(*args):
        return kernel(
            *[
                pltpu.with_memory_space_constraint(arg, pltpu.HBM) if i in hbm else arg
                for i, arg in enumerate(args)
            ]
        )

    return run


def bf(*shape):
    return jax.ShapeDtypeStruct(shape, BF)


def round_bf(value):
    return value.astype(BF).astype(F32)


def lane_index(shape):
    return lax.broadcasted_iota(jnp.int32, shape, len(shape) - 1)


def stat_rows(columns):
    rows = columns[0].shape[0]
    lane = lane_index((rows, LANES))
    out = jnp.zeros((rows, LANES), F32)
    for index, column in enumerate(columns):
        out = jnp.where(lane == index, column, out)
    return out


def two_parts(value):
    high = round_bf(value)
    return high, value - high


def start_copies(sources, targets, sems):
    copies = [
        pltpu.make_async_copy(source, target, sems.at[i])
        for i, (source, target) in enumerate(zip(sources, targets))
    ]
    for copy in copies:
        copy.start()
    return copies


def attention_kernel(where_ref, group_ref, *refs):
    sources, refs = refs[:8], refs[-12:]
    out_ref, kept_ref, row_ref = refs[:3]
    targets, sems = refs[3:11], refs[11]
    len_ref, q_ref, tk_ref, k_ref, tv_ref, v_ref, res_ref, gn_ref = targets
    requests, heads, size = q_ref.shape
    halves = [pl.ds(i * requests // 2, requests // 2) for i in range(2)]
    large = [i for i in range(len(targets)) if targets[i] is k_ref or targets[i] is v_ref]
    small = [i for i in range(len(targets)) if i not in large]
    pairs = [(sources[i].at[h], targets[i].at[h]) for i in large for h in halves]
    pairs += [(sources[i], targets[i]) for i in small]
    copies = start_copies(*zip(*pairs), sems)
    keys, values, others = copies[:2], copies[2:4], copies[4:]
    for copy in keys + others:
        copy.wait()
    slots = k_ref.shape[1]
    scale = size ** (-0.5)
    first = where_ref[0] * slots
    owner = where_ref[0] == 0
    contract = (((1,), (1,)), ((), ()))
    slot = first + lane_index((heads, slots))
    scores, valid, fresh = [], [], []
    for b in range(requests):
        q = q_ref[b]
        scores.append(lax.dot_general(q, k_ref[b], contract, preferred_element_type=F32))
        valid.append(jnp.where(slot < len_ref[b], 1.0, 0.0))
        fresh.append(q.astype(F32) * tk_ref[b : b + 1, :].astype(F32))
    valid = jnp.concatenate(valid, 0) > 0.5
    scores = jnp.where(valid, jnp.concatenate(scores, 0) * scale, -1e30)
    fresh = jnp.sum(jnp.concatenate(fresh, 0), -1, keepdims=True) * scale
    fresh = jnp.where(owner, fresh, -1e30)
    peak = round_bf(jnp.maximum(jnp.max(scores, -1, keepdims=True), fresh))
    weights = jnp.where(valid, jnp.exp(scores - peak), 0.0)
    own = jnp.where(owner, jnp.exp(fresh - peak), 0.0)
    total = jnp.sum(weights, -1, keepdims=True) + own
    rounded = weights.astype(BF)
    own = round_bf(own)
    stats = stat_rows((peak,) + two_parts(total)).astype(BF)
    for copy in values:
        copy.wait()
    for b in range(requests):
        rows = slice(b * heads, (b + 1) * heads)
        acc = jnp.dot(rounded[rows], v_ref[b], preferred_element_type=F32)
        acc = acc + own[rows] * tv_ref[b : b + 1, :].astype(F32)
        out_ref[b, :, :size] = acc.astype(BF)
        out_ref[b, :, size:] = stats[rows]
    kept_ref[...] = res_ref[...]
    gain = gn_ref[...].astype(F32)
    row_ref[...] = jnp.concatenate([gain[i : i + 1] for i in range(gain.shape[0])], -1)


def merge_kernel(got_ref, out_ref):
    size = out_ref.shape[-1]
    stats = got_ref[:, :, size:].astype(F32)
    peak = stats[:, :, 0:1]
    factor = jnp.exp(peak - jnp.max(peak, 0, keepdims=True))
    total = jnp.sum((stats[:, :, 1:2] + stats[:, :, 2:3]) * factor, 0)
    acc = jnp.sum(got_ref[:, :, :size].astype(F32) * factor, 0)
    out_ref[...] = jnp.broadcast_to((acc / total).astype(BF)[None], out_ref.shape)


def project_kernel(got_ref, weight_ref, attended_ref, out_ref, rows_ref):
    requests = attended_ref.shape[0]
    heads = rows_ref.shape[0] // requests
    rows_ref[...] = got_ref[...].astype(F32).reshape(rows_ref.shape)
    attended = jnp.concatenate(
        [rows_ref[pl.ds(h, requests, stride=heads), :].astype(BF) for h in range(heads)], -1
    )
    attended_ref[...] = attended
    projected = jnp.dot(attended, weight_ref[...], preferred_element_type=F32)
    out_ref[...] = projected.astype(BF)


def gate_up_kernel(
    where_ref, p0_ref, p1_ref, p2_ref, p3_ref, residual_ref, gain_ref, gate_ref, up_ref,
    attended_ref, middle_ref, out_ref, result_ref, rows_ref, slots_ref, sems,
):
    writes = start_copies([attended_ref], [result_ref], sems)
    pieces, depth, _ = out_ref.shape
    requests = residual_ref.shape[0]
    halves = pieces // requests
    projected = sum_in_order(where_ref, (p0_ref, p1_ref, p2_ref, p3_ref), slots_ref)
    middle = (residual_ref[...].astype(F32) + projected).astype(BF)
    middle_ref[...] = middle
    middle = middle.astype(F32)
    square = jnp.sum(middle * middle, -1, keepdims=True)
    scaled = (middle * gain_ref[...]).astype(BF)
    blocks = gate_ref.shape[1] // (halves * LANES)

    def put(row, half, value):
        rows_ref[pl.ds(half * depth + row, requests, stride=halves * depth), :] = value

    for start, weight_ref in ((0, gate_ref), (blocks, up_ref)):
        product = jnp.dot(scaled, weight_ref[...], preferred_element_type=F32)
        for j in range(halves * blocks):
            put(start + j % blocks, j // blocks, product[:, j * LANES : (j + 1) * LANES])
    stats = stat_rows(two_parts(square))
    zeros = jnp.zeros_like(stats)
    for half in range(halves):
        put(2 * blocks, half, stats)
        for row in range(2 * blocks + 1, depth):
            put(row, half, zeros)
    out_ref[...] = rows_ref[...].astype(BF).reshape(out_ref.shape)
    for write in writes:
        write.wait()


def hidden_kernel(blocks, got_ref, out_ref):
    summed = jnp.sum(got_ref[...].astype(F32), 0)
    stats = summed[2 * blocks : 2 * blocks + 1]
    square = stats[:, 0:1] + stats[:, 1:2]
    inverse = lax.rsqrt(square / D + 1e-05)
    gate = summed[:blocks] * inverse
    up = summed[blocks : 2 * blocks] * inverse
    hidden = gate / (1.0 + jnp.exp(-gate)) * up
    pad = jnp.zeros((out_ref.shape[1] - blocks, LANES), F32)
    hidden = jnp.concatenate([hidden, pad], 0).astype(BF)
    out_ref[...] = jnp.broadcast_to(hidden[None], out_ref.shape)


def down_kernel(got_ref, weight_ref, out_ref, rows_ref):
    pieces, depth, _ = got_ref.shape
    requests = out_ref.shape[0]
    halves = pieces // requests
    blocks = weight_ref.shape[0] // (halves * LANES)
    rows_ref[...] = got_ref[...].astype(F32).reshape(rows_ref.shape)
    hidden = jnp.concatenate(
        [
            rows_ref[pl.ds(half * depth + row, requests, stride=halves * depth), :].astype(BF)
            for half in range(halves)
            for row in range(blocks)
        ],
        -1,
    )
    down = jnp.dot(hidden, weight_ref[...], preferred_element_type=F32)
    out_ref[...] = down.astype(BF)


def finish_kernel(where_ref, p0_ref, p1_ref, p2_ref, p3_ref, middle_ref, out_ref, slots_ref):
    down = sum_in_order(where_ref, (p0_ref, p1_ref, p2_ref, p3_ref), slots_ref)
    out_ref[...] = (middle_ref[...].astype(F32) + down).astype(BF)


def add_kernel(a_ref, b_ref, out_ref):
    out_ref[...] = (a_ref[...].astype(F32) + b_ref[...].astype(F32)).astype(BF)


def sum_in_order(where_ref, refs, slots_ref):
    own = where_ref[0] // CORES
    for k, ref in enumerate(refs):
        slots_ref[own ^ k] = ref[...].astype(F32)
    return jnp.sum(slots_ref[...], 0)


def exchange(pieces, axis):
    return lax.all_to_all(pieces, axis, 0, 0)


def swap(value, mask):
    pairs = [(i, i ^ mask) for i in range(lax.axis_size("kvh"))]
    return lax.ppermute(value, "kvh", pairs)


def parts_kvh(value):
    both = call(add_kernel, bf(*value.shape), 2)(value, swap(value, 1))
    return [both] + [swap(both, k * CORES) for k in (1, 2, 3)]


def shards(
    queries,
    token_keys,
    token_values,
    key_cache,
    cached_value_rows,
    lengths,
    residual,
    out_weight,
    norm_gain,
    gate_weight,
    up_weight,
    down_weight,
):
    requests, heads, size = queries.shape
    seq = lax.axis_size("seq")
    group = lax.axis_index("kvh").reshape(1)
    rows = requests * heads // seq
    width = residual.shape[1]
    halves = seq // requests
    blocks = gate_weight.shape[1] // (halves * LANES)
    depth = -(-(2 * blocks + 1) // 16) * 16
    thin = -(-blocks // 16) * 16
    where = lax.axis_index("seq").reshape(1)

    cache = (requests, key_cache.shape[1], size)
    packed, residual, gain = call(
        attention_kernel,
        (
            bf(requests, heads, 2 * size),
            bf(requests, width),
            jax.ShapeDtypeStruct((1, width), F32),
        ),
        13,
        scratch=[
            pltpu.SMEM((requests,), jnp.int32),
            pltpu.VMEM((requests, heads, size), BF),
            pltpu.VMEM((requests, size), BF),
            pltpu.VMEM(cache, BF),
            pltpu.VMEM((requests, size), BF),
            pltpu.VMEM(cache, BF),
            pltpu.VMEM((requests, width), BF),
            pltpu.VMEM((width // LANES, LANES), BF),
            DMA((10,)),
        ],
        smem=(0, 1),
        hbm=range(2, 13),
    )(
        where,
        group,
        lengths,
        queries,
        token_keys.reshape(requests, size),
        key_cache.reshape(cache),
        token_values.reshape(requests, size),
        cached_value_rows.reshape(cache),
        residual,
        norm_gain.reshape(-1, LANES),
        gate_weight,
        up_weight,
        down_weight,
    )
    got = exchange(packed.reshape(seq, rows, 2 * size), "seq")
    merged = call(merge_kernel, bf(seq, rows, size), 1)(got)
    attended, projected = call(
        project_kernel,
        (bf(requests, heads * size), bf(requests, width)),
        2,
        scratch=[pltpu.VMEM((requests * heads, size), F32)],
    )(exchange(merged, "seq"), out_weight)
    middle, pieces, attended = call(
        gate_up_kernel,
        (bf(requests, width), bf(seq, depth, LANES), bf(requests, heads * size)),
        10,
        scratch=[
            pltpu.VMEM((seq * depth, LANES), F32),
            pltpu.VMEM((4, requests, width), F32),
            DMA((1,)),
        ],
        smem=(0,),
        hbm_out=(2,),
    )(group, *parts_kvh(projected), residual, gain, gate_weight, up_weight, attended)
    hidden = call(lambda *refs: hidden_kernel(blocks, *refs), bf(seq, thin, LANES), 1)(
        exchange(pieces, "seq")
    )
    down = call(
        down_kernel,
        bf(requests, width),
        2,
        scratch=[pltpu.VMEM((seq * thin, LANES), F32)],
    )(exchange(hidden, "seq"), down_weight)
    updated = call(
        finish_kernel,
        bf(requests, width),
        6,
        scratch=[pltpu.VMEM((4, requests, width), F32)],
        smem=(0,),
    )(group, *parts_kvh(down), middle)
    return (updated, attended)


def solution(mesh):
    return jax.shard_map(
        shards,
        mesh=mesh,
        in_specs=(
            P(None, "kvh", None),
            P(None, "kvh", None),
            P(None, "kvh", None),
            P(None, "seq", "kvh", None),
            P(None, "seq", "kvh", None),
            P(),
            P(None, "seq"),
            P("kvh", "seq"),
            P("seq"),
            P("seq", "kvh"),
            P("seq", "kvh"),
            P("kvh", "seq"),
        ),
        out_specs=(P(None, "seq"), P(None, "kvh")),
        check_vma=False,
    )
```
